512 devices in a mesh: row: 32 (over z, y_hi), col: 16 (over x, y_lo, core).
Axes of the slice: x: 4, y: 8 (y_hi: 4, y_lo: 2; y = y_hi * 2 + y_lo), z: 8, core: 2. Of those that a mesh axis runs over, the one named last changes fastest.
Arguments:
- constraint: bfloat16 [4096, 24576], P('row', 'col'), may hold values from -0.23925781 to 0.23925781
- pattern: int32 [32, 192], P('row', 'col'), may hold values 0 or 1
- scaling: float32 [24576], P('col'), may hold values from 0.1 to 10
- period: int32 [32], P('row'), may hold values from 0 to 15, never falling along the last dimension, each value on 1 to 4 neighbouring positions
- column_period: int32 [192], P('col'), may hold values from 0 to 15, never falling along the last dimension, each value on 1 to 24 neighbouring positions
- damping: float32 [16], replicated, may hold values from 0.5 to 5
Outputs:
- normal_lower: float32 [4096, 4096], P('col', 'row')
The draws below stay inside these ranges and needn't reach their ends.
Inputs may be any that keep to these rules, and one draw needn't show every extreme that they name: Never falling along the block rows; each period covers 1 to 4 block rows, and at least one covers exactly 4. `column_period`: never falling along the block columns; each period covers 1 to 24 block columns, one exactly that many.
All inputs are finite; a program needn't handle non-finite values. No bound on the sum of `pattern` on one device may be relied on, other than what follows from the above.
Results may differ from the reference program's by a relative error of at most 0.0011.
Values may be sent and summed in bfloat16 or wider, within the bound.
No kernel may reach another device: no remote copies, remote signals or barrier semaphores. Data moves between devices by JAX's collectives and lax.ppermute only.
A program may use at most 64 MiB of HBM per device.

```python
import math
import jax
import jax.numpy as jnp
import numpy as np
from jax import lax

BLK = 128
NBR = 32
NBC = 192
PERIODS = 16
NR = 4096
NC = 24576


def set_ends(values, key, smallest, largest):
    index_at = [jax.random.randint(jax.random.fold_in(key, axis), (), 0, length) for axis, length in enumerate(values.shape)]
    widest = values.shape.index(max(values.shape))
    beside = index_at[:widest] + [(index_at[widest] + 1) % values.shape[widest]] + index_at[widest + 1:]
    return values.at[tuple(index_at)].set(smallest).at[tuple(beside)].set(largest)


def shard_levels(key, extent, split, low, top_value):
    gain = 1.0
    for position, shards_of in split:
        heights = jax.random.uniform(jax.random.fold_in(jax.random.fold_in(key, 6), position), (shards_of,), jnp.float32, low / len(split), top_value / len(split))
        gain = gain * jnp.repeat(jnp.exp(heights), extent[position] // shards_of).reshape((-1,) + (1,) * (len(extent) - 1 - position))
    return gain


def length_profile(count, total, limit, skew):
    loads = [(1 << 20) // math.isqrt(standing ** skew) + 1 for standing in range(2, count + 1)]
    spare, given = total - limit - (count - 1), [1] * (count - 1)
    while spare > 0:
        movable = [i for i in range(count - 1) if given[i] < limit]
        whole, remaining = sum([loads[i] for i in movable]), spare
        for i in movable:
            more = min(limit - given[i], max(1, remaining * loads[i] // whole), spare)
            given[i] = given[i] + more
            spare = spare - more
    return np.array([limit] + given)


def uneven(own_key, number_of, total, most, slope):
    if number_of == 2:
        one = jax.random.randint(own_key, (), max(1, total - most), min(most, total - 1) + 1)
        return jnp.stack([one, total - one])
    lengths = jnp.asarray(length_profile(number_of, total, most, slope), jnp.int32)
    couples = (number_of - 1) // 2
    donor, taker = lengths[1:1 + 2 * couples:2], lengths[2:2 + 2 * couples:2]
    margin = jnp.minimum(donor - 1, most - taker)
    shifted = jax.random.randint(jax.random.fold_in(own_key, 1), (couples,), 0, 1 << 20) % (margin + 1)
    lengths = lengths.at[1:1 + 2 * couples:2].set(donor - shifted).at[2:2 + 2 * couples:2].set(taker + shifted)
    return lengths[jax.random.permutation(jax.random.fold_in(own_key, 2), number_of)]


def gaussian(own_key, dims, spread, limit, pieces=(), held_as=jnp.bfloat16):
    drawn = spread * jax.random.normal(own_key, dims, jnp.float32)
    if pieces:
        drawn = drawn * shard_levels(own_key, dims, pieces, -0.22, 0.18)
    return jnp.clip(drawn, -limit, limit).astype(held_as)


def setup_inputs(seed: int = 0) -> dict:
    arg_keys = jax.random.split(jax.random.key(seed), 7)
    return {
        "constraint": gaussian(arg_keys[0], (NR, NC), (0.5 / NC ** 0.25), 0.23925781, ((0, 32), (1, 16))),
        "pattern": set_ends((jax.random.randint(arg_keys[1], (NBR, NBC), 0, 10) < 1).astype(jnp.int32), jax.random.fold_in(arg_keys[1], 1), 0, 1),
        "scaling": jnp.clip(jnp.exp(math.log(10.0) - 4.6051702 * jax.random.uniform(arg_keys[2], (NC,), jnp.float32) ** shard_levels(arg_keys[2], (NC,), ((0, 16),), -0.2, 0.2)), 0.1, 10.0),
        "period": jnp.searchsorted(jnp.cumsum(uneven(arg_keys[3], PERIODS, NBR, 2 * NBR // PERIODS, 0)), jnp.arange(NBR), side="right").astype(jnp.int32),
        "column_period": jnp.searchsorted(jnp.cumsum(uneven(arg_keys[4], PERIODS, NBC, 2 * NBC // PERIODS, 0)), jnp.arange(NBC), side="right").astype(jnp.int32),
        "damping": jnp.clip(jnp.exp(jax.random.uniform(arg_keys[5], (PERIODS,), jnp.float32, math.log(0.5), math.log(5.0))), 0.5, 5.0),
    }


def reference(constraint, pattern, scaling, period, column_period, damping):
    same = column_period[None, :] == period[:, None]
    before = column_period[None, :] == period[:, None] - 1
    present = jnp.where(same | before | (pattern > 0), 1, 0).astype(jnp.int32)
    expanded = jnp.repeat(jnp.repeat(present, BLK, axis=0), BLK, axis=1)
    masked = constraint * expanded.astype(constraint.dtype)
    scaled = (masked.astype(jnp.float32) * scaling[None, :]).astype(jnp.bfloat16)
    product = lax.dot_general(masked, scaled, (((1,), (1,)), ((), ())), preferred_element_type=jnp.float32)
    index_rows = jnp.arange(NR, dtype=jnp.int32)
    lower_keep = (index_rows // BLK)[:, None] >= (index_rows // BLK)[None, :]
    result = jnp.where(lower_keep, product, jnp.float32(0.0))
    per_block = damping[period]
    per_row = jnp.repeat(per_block, BLK)
    on_diagonal = index_rows[:, None] == index_rows[None, :]
    return result + jnp.where(on_diagonal, per_row[None, :], jnp.float32(0.0))
```

```python
import jax
import jax.numpy as jnp
import numpy as np
from jax import lax
from jax.experimental import pallas as pl
from jax.experimental.pallas import tpu as pltpu
from jax.sharding import Mesh, PartitionSpec as P

ROW = ("z", "yh")
COL = ("x", "yl", "core")
NZ, NY, NX, NL, NK = 8, 4, 4, 2, 2
NR, NCOL = NZ * NY, NX * NL * NK
BLK = 128
KC = 1536

HELD = ((0, 0), (0, 1), (1, 0), (7, 0), (1, 2), (5, 0), (3, 3))


def place(z, y):
    return (z % NZ) * NY + y % NY


def col_distance(a, b):
    ax, al, ak = a // (NL * NK), a // NK % NL, a % NK
    bx, bl, bk = b // (NL * NK), b // NK % NL, b % NK
    dx = abs(ax - bx)
    return min(dx, NX - dx) * 4 + abs(al - bl) * 4 + abs(ak - bk)


def plan():
    chosen = {}
    for t in range(len(HELD)):
        for s in range(t):
            dz, dy = (HELD[t][0] - HELD[s][0]) % NZ, (HELD[t][1] - HELD[s][1]) % NY
            if (dz, dy) not in chosen and (-dz % NZ, -dy % NY) not in chosen:
                chosen[(dz, dy)] = (s, t)
    left = np.zeros((NR, NCOL), np.int32)
    right = np.zeros((NR, NCOL), np.int32)
    sends = ([], [])
    seen = set()
    for z in range(NZ):
        for y in range(NY):
            g = place(z, y)
            todo = []
            for (dz, dy), (s, t) in chosen.items():
                if (dz, dy) == (4, 0) and z >= 4:
                    continue
                if (dz, dy) == (4, 2) and z < 4:
                    continue
                if (dz, dy) == (0, 2) and y >= 2:
                    continue
                a = place(z + HELD[s][0], y + HELD[s][1])
                b = place(z + HELD[t][0], y + HELD[t][1])
                todo.append((a, b, s, t) if a > b else (b, a, t, s))
            free = list(range(NCOL))
            cand = sorted(
                (col_distance(c, blk[0] // 2), i, c) for i, blk in enumerate(todo) for c in free
            )
            slot, used = {}, set()
            for _, i, c in cand:
                if i not in slot and c not in used:
                    slot[i] = c
                    used.add(c)
            for i, (p, q, l, r) in enumerate(todo):
                c = slot[i]
                left[g, c], right[g, c] = l, r
                sends[p % 2].append((g * NCOL + c, q * NCOL + p // 2))
                assert (p, q) not in seen
                seen.add((p, q))
    assert len(seen) == NR * (NR - 1) // 2
    return left, right, sends


def pairs_kernel(left, right, d_ref, *refs):
    rows, out, masked, scaled = refs[:7], refs[7], refs[8], refs[9]
    d = d_ref[...]
    for i in range(7):
        m = rows[i][...]
        masked[i] = m
        scaled[i] = (m.astype(jnp.float32) * d).astype(jnp.bfloat16)
    for c in range(NCOL):
        out[c] = lax.dot_general(
            masked[left[c]], scaled[right[c]], (((1,), (1,)), ((), ())), preferred_element_type=jnp.float32
        )


def diag_kernel(d_ref, m_ref, out):
    m = m_ref[...]
    s = (m.astype(jnp.float32) * d_ref[...]).astype(jnp.bfloat16)
    out[...] = lax.dot_general(m, s, (((1,), (1,)), ((), ())), preferred_element_type=jnp.float32)


def final_kernel(ids, period, damping, even, odd, diag, out):
    row, col = ids[0], ids[1]
    damp = damping[period[0]]
    i = lax.broadcasted_iota(jnp.int32, (BLK, BLK), 0)
    j = lax.broadcasted_iota(jnp.int32, (BLK, BLK), 1)
    full = diag[...] + jnp.where(i == j, damp, 0.0)
    own = row // 2 == col
    out[0:BLK] = jnp.where(own & (row % 2 == 0), full, even[...])
    out[BLK : 2 * BLK] = jnp.where(own & (row % 2 == 1), full, odd[...])


def body(constraint, pattern, scaling, period, column_period, damping):
    left, right, sends = plan()
    row, col = lax.axis_index(ROW), lax.axis_index(COL)
    vmem = pl.BlockSpec(memory_space=pltpu.VMEM)
    smem = pl.BlockSpec(memory_space=pltpu.SMEM)

    same = column_period[None, :] == period[:, None]
    before = column_period[None, :] == period[:, None] - 1
    present = jnp.where(same | before | (pattern > 0), 1, 0).astype(constraint.dtype)
    masked = constraint * jnp.repeat(present, BLK, axis=1)

    held = [masked]
    for dz, dy in HELD[1:]:
        pairs = [(place(z + dz, y + dy), place(z, y)) for z in range(NZ) for y in range(NY)]
        held.append(lax.ppermute(masked, ROW, pairs))

    d = scaling.reshape(1, KC)
    diag = pl.pallas_call(
        diag_kernel,
        out_shape=jax.ShapeDtypeStruct((BLK, BLK), jnp.float32),
        in_specs=[vmem, vmem],
        out_specs=vmem,
        name="diag",
    )(d, masked)
    strips = lax.all_to_all(diag, COL, 0, 0, tiled=True).reshape(NCOL, BLK // NCOL, BLK)
    strip = jnp.sum(strips, axis=0)
    diag = lax.all_to_all(jnp.tile(strip, (NCOL, 1)), COL, 0, 0, tiled=True)

    lt = lax.dynamic_index_in_dim(jnp.asarray(left), row, 0, keepdims=False)
    rt = lax.dynamic_index_in_dim(jnp.asarray(right), row, 0, keepdims=False)
    part = pl.pallas_call(
        pairs_kernel,
        out_shape=jax.ShapeDtypeStruct((NCOL, BLK, BLK), jnp.float32),
        in_specs=[smem, smem] + [vmem] * 8,
        out_specs=vmem,
        scratch_shapes=[pltpu.VMEM((7, BLK, KC), jnp.bfloat16)] * 2,
        compiler_params=pltpu.CompilerParams(vmem_limit_bytes=40 * 2**20),
        name="pairs",
    )(lt, rt, d, *held)

    parts = lax.all_to_all(part.astype(jnp.float16), COL, 0, 0, tiled=True)
    mine = jnp.sum(parts.astype(jnp.float32), axis=0)
    even = lax.ppermute(mine, ROW + COL, sends[0])
    odd = lax.ppermute(mine, ROW + COL, sends[1])
    return pl.pallas_call(
        final_kernel,
        out_shape=jax.ShapeDtypeStruct((2 * BLK, BLK), jnp.float32),
        in_specs=[smem] * 3 + [vmem] * 3,
        out_specs=vmem,
        name="final",
    )(jnp.stack([row, col]), period, damping, even, odd, diag)


def solution(mesh):
    split = Mesh(mesh.devices.reshape(NZ, NY, NX, NL, NK), ROW + COL)
    return jax.shard_map(
        body,
        mesh=split,
        in_specs=(P(ROW, COL), P(ROW, COL), P(COL), P(ROW), P(COL), P()),
        out_specs=P(COL, ROW),
        check_vma=False,
    )
```

```python
import jax
import jax.numpy as jnp
import numpy as np
from jax import lax
from jax.experimental import pallas as pl
from jax.experimental.pallas import tpu as pltpu
from jax.sharding import Mesh, PartitionSpec as P

ROW = ("z", "yh")
COL = ("x", "yl", "core")
NZ, NY, NX, NL, NK = 8, 4, 4, 2, 2
NR, NCOL = NZ * NY, NX * NL * NK
BLK = 128
KC = 1536

HELD = ((0, 0), (0, 1), (1, 0), (0, 3), (5, 0), (0, 2), (2, 0), (4, 0))
SOURCE = (0, 0, 0, 0, 0, 1, 2, 4)
NH = len(HELD)


def place(z, y):
    return (z % NZ) * NY + y % NY


def col_distance(a, b):
    ax, al, ak = a // (NL * NK), a // NK % NL, a % NK
    bx, bl, bk = b // (NL * NK), b // NK % NL, b % NK
    dx = abs(ax - bx)
    return min(dx, NX - dx) * 4 + abs(al - bl) * 4 + abs(ak - bk)


def plan():
    chosen = {}
    for t in range(len(HELD)):
        for s in range(t):
            dz, dy = (HELD[t][0] - HELD[s][0]) % NZ, (HELD[t][1] - HELD[s][1]) % NY
            if (dz, dy) not in chosen and (-dz % NZ, -dy % NY) not in chosen:
                chosen[(dz, dy)] = (s, t)
    left = np.zeros((NR, NCOL), np.int32)
    right = np.zeros((NR, NCOL), np.int32)
    sends = ([], [])
    seen = set()
    for z in range(NZ):
        for y in range(NY):
            g = place(z, y)
            todo = []
            for (dz, dy), (s, t) in chosen.items():
                if (dz, dy) == (4, 0) and z >= 4:
                    continue
                if (dz, dy) == (4, 2) and z < 4:
                    continue
                if (dz, dy) == (0, 2) and y >= 2:
                    continue
                a = place(z + HELD[s][0], y + HELD[s][1])
                b = place(z + HELD[t][0], y + HELD[t][1])
                todo.append((a, b, s, t) if a > b else (b, a, t, s))
            free = list(range(NCOL))
            cand = sorted(
                (col_distance(c, blk[0] // 2), i, c) for i, blk in enumerate(todo) for c in free
            )
            slot, used = {}, set()
            for _, i, c in cand:
                if i not in slot and c not in used:
                    slot[i] = c
                    used.add(c)
            for i, (p, q, l, r) in enumerate(todo):
                c = slot[i]
                left[g, c], right[g, c] = l, r
                sends[p % 2].append((g * NCOL + c, q * NCOL + p // 2))
                assert (p, q) not in seen
                seen.add((p, q))
    assert len(seen) == NR * (NR - 1) // 2
    return left, right, sends


def pairs_kernel(left, right, d_ref, *refs):
    rows, (out, masked, scaled) = refs[:NH], refs[NH:]
    d = d_ref[...]
    for i in range(NH):
        m = rows[i][...]
        masked[i] = m
        scaled[i] = (m.astype(jnp.float32) * d).astype(jnp.bfloat16)
    for c in range(NCOL):
        out[c] = lax.dot_general(
            masked[left[c]], scaled[right[c]], (((1,), (1,)), ((), ())), preferred_element_type=jnp.float32
        )


def diag_kernel(d_ref, m_ref, out):
    m = m_ref[...]
    s = (m.astype(jnp.float32) * d_ref[...]).astype(jnp.bfloat16)
    out[...] = lax.dot_general(m, s, (((1,), (1,)), ((), ())), preferred_element_type=jnp.float32)


def final_kernel(ids, period, damping, even, odd, diag, out):
    row, col = ids[0], ids[1]
    damp = damping[period[0]]
    i = lax.broadcasted_iota(jnp.int32, (BLK, BLK), 0)
    j = lax.broadcasted_iota(jnp.int32, (BLK, BLK), 1)
    full = diag[...] + jnp.where(i == j, damp, 0.0)
    own = row // 2 == col
    out[0:BLK] = jnp.where(own & (row % 2 == 0), full, even[...])
    out[BLK : 2 * BLK] = jnp.where(own & (row % 2 == 1), full, odd[...])


def body(constraint, pattern, scaling, period, column_period, damping):
    left, right, sends = plan()
    row, col = lax.axis_index(ROW), lax.axis_index(COL)
    vmem = pl.BlockSpec(memory_space=pltpu.VMEM)
    smem = pl.BlockSpec(memory_space=pltpu.SMEM)

    same = column_period[None, :] == period[:, None]
    before = column_period[None, :] == period[:, None] - 1
    present = jnp.where(same | before | (pattern > 0), 1, 0).astype(constraint.dtype)
    masked = constraint * jnp.repeat(present, BLK, axis=1)

    held = [masked]
    for i in range(1, NH):
        dz, dy = HELD[i][0] - HELD[SOURCE[i]][0], HELD[i][1] - HELD[SOURCE[i]][1]
        pairs = [(place(z + dz, y + dy), place(z, y)) for z in range(NZ) for y in range(NY)]
        held.append(lax.ppermute(held[SOURCE[i]], ROW, pairs))

    d = scaling.reshape(1, KC)
    diag = pl.pallas_call(
        diag_kernel,
        out_shape=jax.ShapeDtypeStruct((BLK, BLK), jnp.float32),
        in_specs=[vmem, vmem],
        out_specs=vmem,
        name="diag",
    )(d, masked)
    strips = lax.all_to_all(diag, COL, 0, 0, tiled=True).reshape(NCOL, BLK // NCOL, BLK)
    strip = jnp.sum(strips, axis=0)
    high = strip.astype(jnp.float16)
    low = (strip - high.astype(jnp.float32)).astype(jnp.float16)
    riders = jnp.broadcast_to(jnp.concatenate([high, low], axis=0), (NCOL, 2 * BLK // NCOL, BLK))

    lt = lax.dynamic_index_in_dim(jnp.asarray(left), row, 0, keepdims=False)
    rt = lax.dynamic_index_in_dim(jnp.asarray(right), row, 0, keepdims=False)
    part = pl.pallas_call(
        pairs_kernel,
        out_shape=jax.ShapeDtypeStruct((NCOL, BLK, BLK), jnp.float32),
        in_specs=[smem, smem] + [vmem] * (1 + NH),
        out_specs=vmem,
        scratch_shapes=[pltpu.VMEM((NH, BLK, KC), jnp.bfloat16)] * 2,
        compiler_params=pltpu.CompilerParams(vmem_limit_bytes=40 * 2**20),
        name="pairs",
    )(lt, rt, d, *held)

    parts = jnp.concatenate([part.astype(jnp.float16), riders], axis=1)
    parts = lax.all_to_all(parts, COL, 0, 0, tiled=True).astype(jnp.float32)
    mine = jnp.sum(parts[:, :BLK], axis=0)
    step = BLK // NCOL
    diag = (parts[:, BLK : BLK + step] + parts[:, BLK + step :]).reshape(BLK, BLK)
    even = lax.ppermute(mine, ROW + COL, sends[0])
    odd = lax.ppermute(mine, ROW + COL, sends[1])
    return pl.pallas_call(
        final_kernel,
        out_shape=jax.ShapeDtypeStruct((2 * BLK, BLK), jnp.float32),
        in_specs=[smem] * 3 + [vmem] * 3,
        out_specs=vmem,
        name="final",
    )(jnp.stack([row, col]), period, damping, even, odd, diag)


def solution(mesh):
    split = Mesh(mesh.devices.reshape(NZ, NY, NX, NL, NK), ROW + COL)
    return jax.shard_map(
        body,
        mesh=split,
        in_specs=(P(ROW, COL), P(ROW, COL), P(COL), P(ROW), P(COL), P()),
        out_specs=P(COL, ROW),
        check_vma=False,
    )
```

```python
import jax
import jax.numpy as jnp
import numpy as np
from jax import lax
from jax.experimental import pallas as pl
from jax.experimental.pallas import tpu as pltpu
from jax.sharding import Mesh, PartitionSpec as P

ROW = ("z", "yh")
COL = ("x", "yl", "core")
NZ, NY, NX, NL, NK = 8, 4, 4, 2, 2
NR, NCOL = NZ * NY, NX * NL * NK
BLK = 128
KC = 1536

HELD = ((0, 0), (5, 0), (1, 0), (0, 1), (0, 3), (2, 0), (0, 2), (4, 0))
NH = len(HELD)
EARLY = 5
HALF = NCOL // 2


def place(z, y):
    return (z % NZ) * NY + y % NY


def col_distance(a, b):
    ax, al, ak = a // (NL * NK), a // NK % NL, a % NK
    bx, bl, bk = b // (NL * NK), b // NK % NL, b % NK
    dx = abs(ax - bx)
    return min(dx, NX - dx) * 4 + abs(al - bl) * 4 + abs(ak - bk)


def plan():
    chosen = {}
    for t in range(NH):
        for s in range(t):
            dz, dy = (HELD[t][0] - HELD[s][0]) % NZ, (HELD[t][1] - HELD[s][1]) % NY
            if (dz, dy) not in chosen and (-dz % NZ, -dy % NY) not in chosen:
                chosen[(dz, dy)] = (s, t)
    left = np.zeros((NR, NCOL), np.int32)
    right = np.zeros((NR, NCOL), np.int32)
    sends = ([], [])
    seen = set()
    for z in range(NZ):
        for y in range(NY):
            g = place(z, y)
            early, late, either = [], [], []
            for (dz, dy), (s, t) in chosen.items():
                if (dz, dy) == (4, 0) and z >= 4 or (dz, dy) == (4, 2) and z < 4 or (dz, dy) == (0, 2) and y >= 2:
                    continue
                a = place(z + HELD[s][0], y + HELD[s][1])
                b = place(z + HELD[t][0], y + HELD[t][1])
                pair = (a, b, s, t) if a > b else (b, a, t, s)
                (either if (dz, dy) == (0, 2) else early if t < EARLY else late).append(pair)
            for pair in either:
                (early if len(early) < HALF else late).append(pair)
            assert len(early) <= HALF and len(late) <= HALF
            for base, todo in ((0, early), (1, late)):
                cand = sorted(
                    (col_distance(2 * i + base, blk[0] // 2), n, i) for n, blk in enumerate(todo) for i in range(HALF)
                )
                slot, used = {}, set()
                for _, n, i in cand:
                    if n not in slot and i not in used:
                        slot[n] = i
                        used.add(i)
                for n, (p, q, l, r) in enumerate(todo):
                    left[g, base * HALF + slot[n]], right[g, base * HALF + slot[n]] = l, r
                    sends[p % 2].append((g * NCOL + 2 * slot[n] + base, q * NCOL + p // 2))
                    assert (p, q) not in seen
                    seen.add((p, q))
    assert len(seen) == NR * (NR - 1) // 2
    return left, right, sends


def product(m, s):
    return lax.dot_general(m, s, (((1,), (1,)), ((), ())), preferred_element_type=jnp.float32)


def scale(m, d):
    return (m.astype(jnp.float32) * d).astype(jnp.bfloat16)


def early_kernel(left, right, d_ref, *refs):
    rows, (out, masked, scaled) = refs[:EARLY], refs[EARLY:]
    d = d_ref[...]
    for i in range(EARLY):
        m = rows[i][...]
        masked[i] = m
        scaled[i] = scale(m, d)
    for c in range(HALF):
        out[c] = product(masked[left[c]], scaled[right[c]])


def late_kernel(left, right, d_ref, masked_in, scaled_in, early, riders, *refs):
    rows, (out, masked, scaled) = refs[: NH - EARLY], refs[NH - EARLY :]
    d = d_ref[...]
    for i in range(EARLY):
        masked[i] = masked_in[i]
        scaled[i] = scaled_in[i]
    for i in range(EARLY, NH):
        m = rows[i - EARLY][...]
        masked[i] = m
        scaled[i] = scale(m, d)
    for c in range(HALF):
        out[2 * c, :BLK] = early[c]
        out[2 * c + 1, :BLK] = product(masked[left[HALF + c]], scaled[right[HALF + c]])
    for c in range(NCOL):
        out[c, BLK:] = riders[...]


def diag_kernel(ids, period, damping, d_ref, m_ref, out):
    m = m_ref[...]
    damp = jnp.where(ids[1] == 0, damping[period[0]], 0.0)
    i = lax.broadcasted_iota(jnp.int32, (BLK, BLK), 0)
    j = lax.broadcasted_iota(jnp.int32, (BLK, BLK), 1)
    out[...] = product(m, scale(m, d_ref[...])) + jnp.where(i == j, damp, 0.0)


def final_kernel(ids, even, odd, diag, out):
    row, col = ids[0], ids[1]
    own = row // 2 == col
    out[0:BLK] = jnp.where(own & (row % 2 == 0), diag[...], even[...])
    out[BLK : 2 * BLK] = jnp.where(own & (row % 2 == 1), diag[...], odd[...])


def body(constraint, pattern, scaling, period, column_period, damping):
    left, right, sends = plan()
    row, col = lax.axis_index(ROW), lax.axis_index(COL)
    vmem = pl.BlockSpec(memory_space=pltpu.VMEM)
    smem = pl.BlockSpec(memory_space=pltpu.SMEM)

    same = column_period[None, :] == period[:, None]
    before = column_period[None, :] == period[:, None] - 1
    present = jnp.where(same | before | (pattern > 0), 1, 0).astype(constraint.dtype)
    masked = constraint * jnp.repeat(present, BLK, axis=1)

    def move(x, dz, dy):
        pairs = [(place(z + dz, y + dy), place(z, y)) for z in range(NZ) for y in range(NY)]
        return lax.ppermute(x, ROW, pairs)

    held = [masked] + [move(masked, *at) for at in HELD[1:EARLY]]
    held.append(move(held[2], 1, 0))
    core = lax.axis_index("core")
    hops = [
        (place(z, y + 1 - 2 * k) * 2 + k, place(z, y) * 2 + k) for z in range(NZ) for y in range(NY) for k in range(2)
    ]
    held.append(lax.ppermute(jnp.where(core == 0, held[3], held[4]), ROW + ("core",), hops))
    held.append(move(held[1], -1, 0))

    small = pltpu.CompilerParams(vmem_limit_bytes=4 * 2**20)
    d = scaling.reshape(1, KC)
    ids = jnp.stack([row, col])
    diag = pl.pallas_call(
        diag_kernel,
        out_shape=jax.ShapeDtypeStruct((BLK, BLK), jnp.float32),
        in_specs=[smem] * 3 + [vmem] * 2,
        out_specs=vmem,
        compiler_params=small,
        name="diag",
    )(ids, period, damping, d, masked)
    strips = lax.all_to_all(diag, COL, 0, 0, tiled=True).reshape(NCOL, BLK // NCOL, BLK)
    strip = jnp.sum(strips, axis=0)
    high = lax.reduce_precision(strip, 5, 10)
    riders = jnp.concatenate([high, strip - high], axis=0)

    lt = lax.dynamic_index_in_dim(jnp.asarray(left), row, 0, keepdims=False)
    rt = lax.dynamic_index_in_dim(jnp.asarray(right), row, 0, keepdims=False)
    stack = jax.ShapeDtypeStruct((EARLY, BLK, KC), jnp.bfloat16)
    sums = jax.ShapeDtypeStruct((HALF, BLK, BLK), jnp.float32)
    params = pltpu.CompilerParams(vmem_limit_bytes=20 * 2**20)
    early, masked_rows, scaled_rows = pl.pallas_call(
        early_kernel,
        out_shape=(sums, stack, stack),
        in_specs=[smem] * 2 + [vmem] * (1 + EARLY),
        out_specs=(vmem,) * 3,
        compiler_params=params,
        name="early",
    )(lt, rt, d, *held[:EARLY])
    parts = pl.pallas_call(
        late_kernel,
        out_shape=jax.ShapeDtypeStruct((NCOL, BLK + 2 * BLK // NCOL, BLK), jnp.float32),
        in_specs=[smem] * 2 + [vmem] * (5 + NH - EARLY),
        out_specs=vmem,
        scratch_shapes=[pltpu.VMEM((NH, BLK, KC), jnp.bfloat16)] * 2,
        compiler_params=params,
        name="late",
    )(lt, rt, d, masked_rows, scaled_rows, early, riders, *held[EARLY:])
    parts = parts.astype(jnp.float16)
    parts = lax.all_to_all(parts, COL, 0, 0, tiled=True).astype(jnp.float32)
    mine = jnp.sum(parts[:, :BLK], axis=0)
    step = BLK // NCOL
    diag = (parts[:, BLK : BLK + step] + parts[:, BLK + step :]).reshape(BLK, BLK)
    even = lax.ppermute(mine, ROW + COL, sends[0])
    odd = lax.ppermute(mine, ROW + COL, sends[1])
    return pl.pallas_call(
        final_kernel,
        out_shape=jax.ShapeDtypeStruct((2 * BLK, BLK), jnp.float32),
        in_specs=[smem] + [vmem] * 3,
        out_specs=vmem,
        compiler_params=small,
        name="final",
    )(ids, even, odd, diag)


def solution(mesh):
    split = Mesh(mesh.devices.reshape(NZ, NY, NX, NL, NK), ROW + COL)
    return jax.shard_map(
        body,
        mesh=split,
        in_specs=(P(ROW, COL), P(ROW, COL), P(COL), P(ROW), P(COL), P()),
        out_specs=P(COL, ROW),
        check_vma=False,
    )
```

```python
import jax
import jax.numpy as jnp
import numpy as np
from jax import lax
from jax.experimental import pallas as pl
from jax.experimental.pallas import tpu as pltpu
from jax.sharding import Mesh, PartitionSpec as P

ROW = ("z", "yh")
COL = ("x", "yl", "core")
NZ, NY, NX, NL, NK = 8, 4, 4, 2, 2
NR, NCOL = NZ * NY, NX * NL * NK
BLK = 128
KC = 1536

HELD = ((0, 0), (6, 0), (1, 0), (0, 1), (0, 3), (3, 0), (0, 2), (4, 0))
NH = len(HELD)
EARLY = 5
HALF = NCOL // 2


def place(z, y):
    return (z % NZ) * NY + y % NY


def col_distance(a, b):
    ax, al, ak = a // (NL * NK), a // NK % NL, a % NK
    bx, bl, bk = b // (NL * NK), b // NK % NL, b % NK
    dx = abs(ax - bx)
    return min(dx, NX - dx) * 4 + abs(al - bl) * 4 + abs(ak - bk)


def plan():
    chosen = {}
    for t in range(NH):
        for s in range(t):
            dz, dy = (HELD[t][0] - HELD[s][0]) % NZ, (HELD[t][1] - HELD[s][1]) % NY
            if (dz, dy) not in chosen and (-dz % NZ, -dy % NY) not in chosen:
                chosen[(dz, dy)] = (s, t)
    left = np.zeros((NR, NCOL), np.int32)
    right = np.zeros((NR, NCOL), np.int32)
    sends = ([], [])
    seen = set()
    for z in range(NZ):
        for y in range(NY):
            g = place(z, y)
            early, late = [], []
            for (dz, dy), (s, t) in chosen.items():
                if (dz, dy) == (4, 0) and z >= 4 or (dz, dy) == (4, 2) and z < 4 or (dz, dy) == (0, 2) and y >= 2:
                    continue
                a = place(z + HELD[s][0], y + HELD[s][1])
                b = place(z + HELD[t][0], y + HELD[t][1])
                pair = (a, b, s, t) if a > b else (b, a, t, s)
                (early if t < EARLY and (dz, dy) != (0, 2) else late).append(pair)
            assert len(early) <= HALF and len(late) <= HALF
            for base, todo in ((0, early), (1, late)):
                cand = sorted(
                    (col_distance(2 * i + base, blk[0] // 2), n, i) for n, blk in enumerate(todo) for i in range(HALF)
                )
                slot, used = {}, set()
                for _, n, i in cand:
                    if n not in slot and i not in used:
                        slot[n] = i
                        used.add(i)
                for n, (p, q, l, r) in enumerate(todo):
                    left[g, base * HALF + slot[n]], right[g, base * HALF + slot[n]] = l, r
                    sends[p % 2].append((g * NCOL + 2 * slot[n] + base, q * NCOL + p // 2))
                    assert (p, q) not in seen
                    seen.add((p, q))
    assert len(seen) == NR * (NR - 1) // 2
    return left, right, sends


def product(m, s):
    return lax.dot_general(m, s, (((1,), (1,)), ((), ())), preferred_element_type=jnp.float32)


def scale(m, d):
    return (m.astype(jnp.float32) * d).astype(jnp.bfloat16)


def early_kernel(left, right, d_ref, *refs):
    rows, (out, masked, scaled) = refs[:EARLY], refs[EARLY:]
    d = d_ref[...]
    for i in range(EARLY):
        m = rows[i][...]
        masked[i] = m
        scaled[i] = scale(m, d)
    for c in range(HALF):
        out[c] = product(masked[left[c]], scaled[right[c]])


def late_kernel(left, right, d_ref, masked_in, scaled_in, early, riders, *refs):
    rows, (out, masked, scaled) = refs[: NH - EARLY], refs[NH - EARLY :]
    d = d_ref[...]
    for i in range(EARLY):
        masked[i] = masked_in[i]
        scaled[i] = scaled_in[i]
    for i in range(EARLY, NH):
        m = rows[i - EARLY][...]
        masked[i] = m
        scaled[i] = scale(m, d)
    for c in range(HALF):
        out[2 * c, :BLK] = early[c]
        out[2 * c + 1, :BLK] = product(masked[left[HALF + c]], scaled[right[HALF + c]])
    for c in range(NCOL):
        out[c, BLK:] = riders[...]


def diag_kernel(ids, period, damping, d_ref, m_ref, out):
    m = m_ref[...]
    damp = jnp.where(ids[1] == 0, damping[period[0]], 0.0)
    i = lax.broadcasted_iota(jnp.int32, (BLK, BLK), 0)
    j = lax.broadcasted_iota(jnp.int32, (BLK, BLK), 1)
    out[...] = product(m, scale(m, d_ref[...])) + jnp.where(i == j, damp, 0.0)


def final_kernel(ids, even, odd, diag, out):
    row, col = ids[0], ids[1]
    own = row // 2 == col
    out[0:BLK] = jnp.where(own & (row % 2 == 0), diag[...], even[...])
    out[BLK : 2 * BLK] = jnp.where(own & (row % 2 == 1), diag[...], odd[...])


def body(constraint, pattern, scaling, period, column_period, damping):
    left, right, sends = plan()
    row, col = lax.axis_index(ROW), lax.axis_index(COL)
    vmem = pl.BlockSpec(memory_space=pltpu.VMEM)
    smem = pl.BlockSpec(memory_space=pltpu.SMEM)

    same = column_period[None, :] == period[:, None]
    before = column_period[None, :] == period[:, None] - 1
    present = jnp.where(same | before | (pattern > 0), 1, 0).astype(constraint.dtype)
    masked = constraint * jnp.repeat(present, BLK, axis=1)

    def move(x, dz, dy):
        pairs = [(place(z + dz, y + dy), place(z, y)) for z in range(NZ) for y in range(NY)]
        return lax.ppermute(x, ROW, pairs)

    held = [masked] + [move(masked, *at) for at in HELD[1:EARLY]]
    held.append(move(held[2], 2, 0))
    core = lax.axis_index("core")
    hops = [
        (place(z, y + 1 - 2 * k) * 2 + k, place(z, y) * 2 + k) for z in range(NZ) for y in range(NY) for k in range(2)
    ]
    held.append(lax.ppermute(jnp.where(core == 0, held[3], held[4]), ROW + ("core",), hops))
    held.append(move(jnp.where(core < 2, held[1], held[4]), -2, 0))

    small = pltpu.CompilerParams(vmem_limit_bytes=4 * 2**20)
    d = scaling.reshape(1, KC)
    ids = jnp.stack([row, col])
    diag = pl.pallas_call(
        diag_kernel,
        out_shape=jax.ShapeDtypeStruct((BLK, BLK), jnp.float32),
        in_specs=[smem] * 3 + [vmem] * 2,
        out_specs=vmem,
        compiler_params=small,
        name="diag",
    )(ids, period, damping, d, masked)
    strips = lax.all_to_all(diag, COL, 0, 0, tiled=True).reshape(NCOL, BLK // NCOL, BLK)
    strip = jnp.sum(strips, axis=0)
    high = lax.reduce_precision(strip, 5, 10)
    riders = jnp.concatenate([high, strip - high], axis=0)

    lt = lax.dynamic_index_in_dim(jnp.asarray(left), row, 0, keepdims=False)
    rt = lax.dynamic_index_in_dim(jnp.asarray(right), row, 0, keepdims=False)
    stack = jax.ShapeDtypeStruct((EARLY, BLK, KC), jnp.bfloat16)
    sums = jax.ShapeDtypeStruct((HALF, BLK, BLK), jnp.float32)
    params = pltpu.CompilerParams(vmem_limit_bytes=20 * 2**20)
    early, masked_rows, scaled_rows = pl.pallas_call(
        early_kernel,
        out_shape=(sums, stack, stack),
        in_specs=[smem] * 2 + [vmem] * (1 + EARLY),
        out_specs=(vmem,) * 3,
        compiler_params=params,
        name="early",
    )(lt, rt, d, *held[:EARLY])
    parts = pl.pallas_call(
        late_kernel,
        out_shape=jax.ShapeDtypeStruct((NCOL, BLK + 2 * BLK // NCOL, BLK), jnp.float32),
        in_specs=[smem] * 2 + [vmem] * (5 + NH - EARLY),
        out_specs=vmem,
        scratch_shapes=[pltpu.VMEM((NH, BLK, KC), jnp.bfloat16)] * 2,
        compiler_params=params,
        name="late",
    )(lt, rt, d, masked_rows, scaled_rows, early, riders, *held[EARLY:])
    parts = parts.astype(jnp.float16)
    parts = lax.all_to_all(parts, COL, 0, 0, tiled=True).astype(jnp.float32)
    mine = jnp.sum(parts[:, :BLK], axis=0)
    step = BLK // NCOL
    diag = (parts[:, BLK : BLK + step] + parts[:, BLK + step :]).reshape(BLK, BLK)
    even = lax.ppermute(mine, ROW + COL, sends[0])
    odd = lax.ppermute(mine, ROW + COL, sends[1])
    return pl.pallas_call(
        final_kernel,
        out_shape=jax.ShapeDtypeStruct((2 * BLK, BLK), jnp.float32),
        in_specs=[smem] + [vmem] * 3,
        out_specs=vmem,
        compiler_params=small,
        name="final",
    )(ids, even, odd, diag)


def solution(mesh):
    split = Mesh(mesh.devices.reshape(NZ, NY, NX, NL, NK), ROW + COL)
    return jax.shard_map(
        body,
        mesh=split,
        in_specs=(P(ROW, COL), P(ROW, COL), P(COL), P(ROW), P(COL), P()),
        out_specs=P(COL, ROW),
        check_vma=False,
    )
```

```python
import jax
import jax.numpy as jnp
import numpy as np
from jax import lax
from jax.experimental import pallas as pl
from jax.experimental.pallas import tpu as pltpu
from jax.sharding import Mesh, PartitionSpec as P

ROW = ("z", "yh")
COL = ("x", "yl", "core")
NZ, NY, NX, NL, NK = 8, 4, 4, 2, 2
NR, NCOL = NZ * NY, NX * NL * NK
BLK = 128
KC = 1536

HELD = ((0, 0), (1, 0), (5, 0), (0, 1), (0, 3), (2, 0), (4, 0), (0, 2))
NH = len(HELD)
SWAP = (0, 1, 2, 4, 3, 5, 6, 7)
EARLY = 5
HALF = NCOL // 2


def place(z, y):
    return (z % NZ) * NY + y % NY


def col_distance(a, b):
    ax, al, ak = a // (NL * NK), a // NK % NL, a % NK
    bx, bl, bk = b // (NL * NK), b // NK % NL, b % NK
    dx = abs(ax - bx)
    return min(dx, NX - dx) * 4 + abs(al - bl) * 4 + abs(ak - bk)


def plan():
    chosen = {}
    for t in range(NH):
        for s in range(t):
            dz, dy = (HELD[t][0] - HELD[s][0]) % NZ, (HELD[t][1] - HELD[s][1]) % NY
            if (dz, dy) not in chosen and (-dz % NZ, -dy % NY) not in chosen:
                chosen[(dz, dy)] = (s, t)
    left = np.zeros((NR, NCOL), np.int32)
    right = np.zeros((NR, NCOL), np.int32)
    sends = ([], [])
    seen = set()
    for z in range(NZ):
        for y in range(NY):
            g = place(z, y)
            early, late, either = [], [], []
            for (dz, dy), (s, t) in chosen.items():
                if (dz, dy) == (4, 0) and z >= 4 or (dz, dy) == (4, 2) and z < 4 or (dz, dy) == (0, 2) and y >= 2:
                    continue
                a = place(z + HELD[s][0], y + HELD[s][1])
                b = place(z + HELD[t][0], y + HELD[t][1])
                pair = (a, b, s, t) if a > b else (b, a, t, s)
                (either if (dz, dy) == (0, 2) else early if t < EARLY else late).append(pair)
            for pair in either:
                (early if len(early) < HALF else late).append(pair)
            assert len(early) <= HALF and len(late) <= HALF
            for base, todo in ((0, early), (1, late)):
                cand = sorted(
                    (col_distance(2 * i + base, blk[0] // 2), n, i) for n, blk in enumerate(todo) for i in range(HALF)
                )
                slot, used = {}, set()
                for _, n, i in cand:
                    if n not in slot and i not in used:
                        slot[n] = i
                        used.add(i)
                for n, (p, q, l, r) in enumerate(todo):
                    left[g, base * HALF + slot[n]], right[g, base * HALF + slot[n]] = l, r
                    sends[p % 2].append((g * NCOL + 2 * slot[n] + base, q * NCOL + p // 2))
                    assert (p, q) not in seen
                    seen.add((p, q))
    assert len(seen) == NR * (NR - 1) // 2
    swap = np.asarray(SWAP, np.int32)
    return np.stack([left, swap[left]], 1), np.stack([right, swap[right]], 1), sends


def product(m, s):
    return lax.dot_general(m, s, (((1,), (1,)), ((), ())), preferred_element_type=jnp.float32)


def scale(m, d):
    return (m.astype(jnp.float32) * d).astype(jnp.bfloat16)


def early_kernel(left, right, d_ref, *refs):
    rows, (out, masked, scaled) = refs[:EARLY], refs[EARLY:]
    d = d_ref[...]
    for i in range(EARLY):
        m = rows[i][...]
        masked[i] = m
        scaled[i] = scale(m, d)
    for c in range(HALF):
        out[c] = product(masked[left[c]], scaled[right[c]])


def late_kernel(left, right, d_ref, masked_in, scaled_in, early, riders, *refs):
    rows, (out, masked, scaled) = refs[: NH - EARLY], refs[NH - EARLY :]
    d = d_ref[...]
    for i in range(EARLY):
        masked[i] = masked_in[i]
        scaled[i] = scaled_in[i]
    for i in range(EARLY, NH):
        m = rows[i - EARLY][...]
        masked[i] = m
        scaled[i] = scale(m, d)
    for c in range(HALF):
        out[2 * c, :BLK] = early[c]
        out[2 * c + 1, :BLK] = product(masked[left[HALF + c]], scaled[right[HALF + c]])
    for c in range(NCOL):
        out[c, BLK:] = riders[...]


def diag_kernel(ids, period, damping, d_ref, m_ref, out):
    m = m_ref[...]
    damp = jnp.where(ids[1] == 0, damping[period[0]], 0.0)
    i = lax.broadcasted_iota(jnp.int32, (BLK, BLK), 0)
    j = lax.broadcasted_iota(jnp.int32, (BLK, BLK), 1)
    out[...] = product(m, scale(m, d_ref[...])) + jnp.where(i == j, damp, 0.0)


def final_kernel(ids, even, odd, diag, out):
    row, col = ids[0], ids[1]
    own = row // 2 == col
    out[0:BLK] = jnp.where(own & (row % 2 == 0), diag[...], even[...])
    out[BLK : 2 * BLK] = jnp.where(own & (row % 2 == 1), diag[...], odd[...])


def body(constraint, pattern, scaling, period, column_period, damping):
    left, right, sends = plan()
    row, col = lax.axis_index(ROW), lax.axis_index(COL)
    vmem = pl.BlockSpec(memory_space=pltpu.VMEM)
    smem = pl.BlockSpec(memory_space=pltpu.SMEM)

    same = column_period[None, :] == period[:, None]
    before = column_period[None, :] == period[:, None] - 1
    present = jnp.where(same | before | (pattern > 0), 1, 0).astype(constraint.dtype)
    masked = constraint * jnp.repeat(present, BLK, axis=1)

    def move(x, dz, dy):
        pairs = [
            (place(z + dz, y + (1 - 2 * k) * dy) * 2 + k, place(z, y) * 2 + k)
            for z in range(NZ)
            for y in range(NY)
            for k in range(2)
        ]
        return lax.ppermute(x, ROW + ("core",), pairs)

    held = [masked] + [move(masked, *at) for at in HELD[1:EARLY]]
    held += [move(held[1], 1, 0), move(held[2], -1, 0), move(held[3], 0, 1)]

    small = pltpu.CompilerParams(vmem_limit_bytes=4 * 2**20)
    d = scaling.reshape(1, KC)
    ids = jnp.stack([row, col])
    diag = pl.pallas_call(
        diag_kernel,
        out_shape=jax.ShapeDtypeStruct((BLK, BLK), jnp.float32),
        in_specs=[smem] * 3 + [vmem] * 2,
        out_specs=vmem,
        compiler_params=small,
        name="diag",
    )(ids, period, damping, d, masked)
    strips = lax.all_to_all(diag, COL, 0, 0, tiled=True).reshape(NCOL, BLK // NCOL, BLK)
    strip = jnp.sum(strips, axis=0)
    high = lax.reduce_precision(strip, 5, 10)
    riders = jnp.concatenate([high, strip - high], axis=0)

    lt = lax.dynamic_slice(jnp.asarray(left), (row, lax.axis_index("core"), 0), (1, 1, NCOL)).reshape(NCOL)
    rt = lax.dynamic_slice(jnp.asarray(right), (row, lax.axis_index("core"), 0), (1, 1, NCOL)).reshape(NCOL)
    stack = jax.ShapeDtypeStruct((EARLY, BLK, KC), jnp.bfloat16)
    sums = jax.ShapeDtypeStruct((HALF, BLK, BLK), jnp.float32)
    params = pltpu.CompilerParams(vmem_limit_bytes=20 * 2**20)
    early, masked_rows, scaled_rows = pl.pallas_call(
        early_kernel,
        out_shape=(sums, stack, stack),
        in_specs=[smem] * 2 + [vmem] * (1 + EARLY),
        out_specs=(vmem,) * 3,
        compiler_params=params,
        name="early",
    )(lt, rt, d, *held[:EARLY])
    parts = pl.pallas_call(
        late_kernel,
        out_shape=jax.ShapeDtypeStruct((NCOL, BLK + 2 * BLK // NCOL, BLK), jnp.float32),
        in_specs=[smem] * 2 + [vmem] * (5 + NH - EARLY),
        out_specs=vmem,
        scratch_shapes=[pltpu.VMEM((NH, BLK, KC), jnp.bfloat16)] * 2,
        compiler_params=params,
        name="late",
    )(lt, rt, d, masked_rows, scaled_rows, early, riders, *held[EARLY:])
    parts = parts.astype(jnp.float16)
    parts = lax.all_to_all(parts, COL, 0, 0, tiled=True).astype(jnp.float32)
    mine = jnp.sum(parts[:, :BLK], axis=0)
    step = BLK // NCOL
    diag = (parts[:, BLK : BLK + step] + parts[:, BLK + step :]).reshape(BLK, BLK)
    even = lax.ppermute(mine, ROW + COL, sends[0])
    odd = lax.ppermute(mine, ROW + COL, sends[1])
    return pl.pallas_call(
        final_kernel,
        out_shape=jax.ShapeDtypeStruct((2 * BLK, BLK), jnp.float32),
        in_specs=[smem] + [vmem] * 3,
        out_specs=vmem,
        compiler_params=small,
        name="final",
    )(ids, even, odd, diag)


def solution(mesh):
    split = Mesh(mesh.devices.reshape(NZ, NY, NX, NL, NK), ROW + COL)
    return jax.shard_map(
        body,
        mesh=split,
        in_specs=(P(ROW, COL), P(ROW, COL), P(COL), P(ROW), P(COL), P()),
        out_specs=P(COL, ROW),
        check_vma=False,
    )
```

```python
import jax
import jax.numpy as jnp
import numpy as np
from jax import lax
from jax.experimental import pallas as pl
from jax.experimental.pallas import tpu as pltpu
from jax.sharding import Mesh, PartitionSpec as P

ROW = ("z", "yh")
CHIP = ("x", "yl")
COL = CHIP + ("core",)
NZ, NY, NX, NL, NK = 8, 4, 4, 2, 2
NR, NCHIP, NCOL = NZ * NY, NX * NL, NX * NL * NK
BLK = 128
KC = 1536
STEP = BLK // NCOL

HELD = ((0, 0), (2, 0), (0, 1), (1, 0), (0, 3), (4, 0), (0, 2), (3, 0))
NH = len(HELD)
EARLY = 5
NSEND = 4


def place(z, y):
    return (z % NZ) * NY + y % NY


def chip_distance(a, b):
    dx = abs(a // NL - b // NL)
    return min(dx, NX - dx) + abs(a % NL - b % NL)


def colour(edges):
    at = ([[-1] * NSEND for _ in range(NR * NCOL)], [[-1] * NSEND for _ in range(NR * NCOL)])
    colours = [-1] * len(edges)
    for e, ends in enumerate(edges):
        a = at[0][ends[0]].index(-1)
        b = at[1][ends[1]].index(-1)
        path, side, node, want = [], 1, ends[1], a
        while at[side][node][want] >= 0:
            f = at[side][node][want]
            path.append(f)
            side = 1 - side
            node = edges[f][side]
            want = a + b - want
        for f in path:
            for s in (0, 1):
                at[s][edges[f][s]][colours[f]] = -1
        for f in path:
            colours[f] = a + b - colours[f]
        colours[e] = a
        for f in path + [e]:
            for s in (0, 1):
                at[s][edges[f][s]][colours[f]] = f
    return colours


def plan():
    chosen = {}
    for t in range(NH):
        for s in range(t):
            dz, dy = (HELD[t][0] - HELD[s][0]) % NZ, (HELD[t][1] - HELD[s][1]) % NY
            if (dz, dy) not in chosen and (-dz % NZ, -dy % NY) not in chosen:
                chosen[(dz, dy)] = (s, t)
    table = np.zeros((NR * NCOL, 4 * NCHIP + 2 * NSEND), np.int32)
    edges, marks = [], []
    for k in range(NK):
        seen = set()
        for z in range(NZ):
            for y in range(NY):
                g = place(z, y)
                kinds = ([], [])
                for (dz, dy), (s, t) in chosen.items():
                    if (dz, dy) == (4, 0) and z >= 4 or (dz, dy) == (4, 2) and z < 4 or (dz, dy) == (0, 2) and y >= 2:
                        continue
                    a = place(z + (1 - 2 * k) * HELD[s][0], y + (1 - 2 * k) * HELD[s][1])
                    b = place(z + (1 - 2 * k) * HELD[t][0], y + (1 - 2 * k) * HELD[t][1])
                    kinds[t >= EARLY].append((a, b, s, t) if a > b else (b, a, t, s))
                for kind, todo in enumerate(kinds):
                    assert len(todo) <= NCHIP
                    cand = sorted(
                        (chip_distance(i, blk[0] // 4), n, i) for n, blk in enumerate(todo) for i in range(NCHIP)
                    )
                    slot, used = {}, set()
                    for _, n, i in cand:
                        if n not in slot and i not in used:
                            slot[n] = i
                            used.add(i)
                    for n, (p, q, l, r) in enumerate(todo):
                        for i in range(NCHIP):
                            device = g * NCOL + i * NK + k
                            table[device, kind * NCHIP + slot[n]] = l
                            table[device, (2 + kind) * NCHIP + slot[n]] = r
                        edges.append((g * NCOL + slot[n] * NK + k, q * NCOL + p // 2))
                        marks.append((kind, p % 2))
                        assert (p, q) not in seen
                        seen.add((p, q))
        assert len(seen) == NR * (NR - 1) // 2
    sends = [[] for _ in range(NSEND)]
    for (source, owner), (kind, half), c in zip(edges, marks, colour(edges)):
        sends[c].append((source, owner))
        table[source, 4 * NCHIP + c] = kind
        table[owner, 4 * NCHIP + NSEND + c] = half
    return table, sends


def product(m, s):
    return lax.dot_general(m, s, (((1,), (1,)), ((), ())), preferred_element_type=jnp.float32)


def scale(m, d):
    return (m.astype(jnp.float32) * d).astype(jnp.bfloat16)


def early_kernel(table, d_ref, *refs):
    rows, (out, masked, scaled) = refs[:EARLY], refs[EARLY:]
    d = d_ref[...]
    for i in range(EARLY):
        m = rows[i][...]
        masked[i] = m
        scaled[i] = scale(m, d)
    for c in range(NCHIP):
        out[c] = product(masked[table[c]], scaled[table[2 * NCHIP + c]])


def late_kernel(table, d_ref, masked_in, scaled_in, early, riders, *refs):
    rows, (out, masked, scaled) = refs[: NH - EARLY], refs[NH - EARLY :]
    d = d_ref[...]
    for i in range(EARLY):
        masked[i] = masked_in[i]
        scaled[i] = scaled_in[i]
    for i in range(EARLY, NH):
        m = rows[i - EARLY][...]
        masked[i] = m
        scaled[i] = scale(m, d)
    for c in range(NCHIP):
        out[c, :BLK] = early[c]
        out[c, BLK : 2 * BLK] = product(masked[table[NCHIP + c]], scaled[table[3 * NCHIP + c]])
        out[c, 2 * BLK :] = riders[...]


def diag_kernel(ids, period, damping, d_ref, m_ref, out):
    m = m_ref[...]
    damp = jnp.where(ids[1] == 0, damping[period[0]], 0.0)
    i = lax.broadcasted_iota(jnp.int32, (BLK, BLK), 0)
    j = lax.broadcasted_iota(jnp.int32, (BLK, BLK), 1)
    out[...] = product(m, scale(m, d_ref[...])) + jnp.where(i == j, damp, 0.0)


def pick_kernel(table, sums, *outs):
    for c in range(NSEND):
        outs[c][...] = jnp.where(table[4 * NCHIP + c] == 1, sums[BLK:], sums[:BLK])


def final_kernel(ids, table, near, far, *refs):
    got, (out, diag) = refs[:NSEND], refs[NSEND:]
    row, col = ids[0], ids[1]
    own = row // 2 == col
    first = col % NK == 0
    for i in range(NCHIP):
        diag[2 * i * STEP : (2 * i + 1) * STEP] = jnp.where(first, near[i], far[i])
        diag[(2 * i + 1) * STEP : (2 * i + 2) * STEP] = jnp.where(first, far[i], near[i])
    for half in range(2):
        total = jnp.where(own & (row % 2 == half), diag[...], 0.0)
        for c in range(NSEND):
            total = total + jnp.where(table[4 * NCHIP + NSEND + c] == half, got[c][...], 0.0)
        out[half * BLK : (half + 1) * BLK] = total


def body(constraint, pattern, scaling, period, column_period, damping):
    table, sends = plan()
    row, col = lax.axis_index(ROW), lax.axis_index(COL)
    vmem = pl.BlockSpec(memory_space=pltpu.VMEM)
    smem = pl.BlockSpec(memory_space=pltpu.SMEM)
    small = pltpu.CompilerParams(vmem_limit_bytes=4 * 2**20)
    large = pltpu.CompilerParams(vmem_limit_bytes=20 * 2**20)
    block = jax.ShapeDtypeStruct((BLK, BLK), jnp.float32)

    same = column_period[None, :] == period[:, None]
    before = column_period[None, :] == period[:, None] - 1
    present = jnp.where(same | before | (pattern > 0), 1, 0).astype(constraint.dtype)
    masked = constraint * jnp.repeat(present, BLK, axis=1)

    def move(x, dz, dy):
        pairs = []
        for z in range(NZ):
            for y in range(NY):
                for k in range(NK):
                    source = place(z + (1 - 2 * k) * dz, y + (1 - 2 * k) * dy)
                    pairs.append((source * NK + k, place(z, y) * NK + k))
        return lax.ppermute(x, ROW + ("core",), pairs)

    held = [masked] + [move(masked, *at) for at in HELD[1:EARLY]]
    held += [move(held[1], 2, 0), move(held[2], 0, 1), move(held[1], 1, 0)]

    d = scaling.reshape(1, KC)
    ids = jnp.stack([row, col])
    mine = lax.dynamic_slice(jnp.asarray(table), (row * NCOL + col, 0), (1, table.shape[1])).reshape(-1)
    diag = pl.pallas_call(
        diag_kernel,
        out_shape=block,
        in_specs=[smem] * 3 + [vmem] * 2,
        out_specs=vmem,
        compiler_params=small,
        name="diag",
    )(ids, period, damping, d, masked)
    strips = lax.all_to_all(diag, COL, 0, 0, tiled=True).reshape(NCOL, STEP, BLK)
    strip = jnp.sum(strips, axis=0)
    high = lax.reduce_precision(strip, 5, 10)
    riders = jnp.concatenate([high, strip - high], axis=0)

    stack = jax.ShapeDtypeStruct((EARLY, BLK, KC), jnp.bfloat16)
    early, masked_rows, scaled_rows = pl.pallas_call(
        early_kernel,
        out_shape=(jax.ShapeDtypeStruct((NCHIP, BLK, BLK), jnp.float32), stack, stack),
        in_specs=[smem] + [vmem] * (1 + EARLY),
        out_specs=(vmem,) * 3,
        compiler_params=large,
        name="early",
    )(mine, d, *held[:EARLY])
    parts = pl.pallas_call(
        late_kernel,
        out_shape=jax.ShapeDtypeStruct((NCHIP, 2 * BLK + 2 * STEP, BLK), jnp.float32),
        in_specs=[smem] + [vmem] * (5 + NH - EARLY),
        out_specs=vmem,
        scratch_shapes=[pltpu.VMEM((NH, BLK, KC), jnp.bfloat16)] * 2,
        compiler_params=large,
        name="late",
    )(mine, d, masked_rows, scaled_rows, early, riders, *held[EARLY:])
    parts = lax.all_to_all(parts.astype(jnp.float16), CHIP, 0, 0, tiled=True).astype(jnp.float32)
    sums = jnp.sum(parts[:, : 2 * BLK], axis=0)
    near = parts[:, 2 * BLK : 2 * BLK + STEP] + parts[:, 2 * BLK + STEP :]
    leaving = pl.pallas_call(
        pick_kernel,
        out_shape=(block,) * NSEND,
        in_specs=[smem, vmem],
        out_specs=(vmem,) * NSEND,
        compiler_params=small,
        name="pick",
    )(mine, sums)
    got = [lax.ppermute(x, ROW + COL, pairs) for x, pairs in zip(leaving, sends)]
    far = lax.ppermute(near, "core", [(0, 1), (1, 0)])
    return pl.pallas_call(
        final_kernel,
        out_shape=jax.ShapeDtypeStruct((2 * BLK, BLK), jnp.float32),
        in_specs=[smem] * 2 + [vmem] * (2 + NSEND),
        out_specs=vmem,
        scratch_shapes=[pltpu.VMEM((BLK, BLK), jnp.float32)],
        compiler_params=small,
        name="final",
    )(ids, mine, near, far, *got)


def solution(mesh):
    split = Mesh(mesh.devices.reshape(NZ, NY, NX, NL, NK), ROW + COL)
    return jax.shard_map(
        body,
        mesh=split,
        in_specs=(P(ROW, COL), P(ROW, COL), P(COL), P(ROW), P(COL), P()),
        out_specs=P(COL, ROW),
        check_vma=False,
    )
```

```python
import jax
import jax.numpy as jnp
import numpy as np
from jax import lax
from jax.experimental import pallas as pl
from jax.experimental.pallas import tpu as pltpu
from jax.sharding import Mesh, PartitionSpec as P

ROW = ("z", "yh")
COL = ("x", "yl", "core")
NZ, NY, NX, NL, NK = 8, 4, 4, 2, 2
NR, NCOL = NZ * NY, NX * NL * NK
BLK = 128
KC = 1536

HELD = ((0, 0), (5, 0), (1, 0), (0, 1), (0, 3), (2, 0), (0, 2), (4, 0))
NH = len(HELD)
SWAP = (0, 1, 2, 4, 3, 5, 6, 7)
EARLY = 5
HALF = NCOL // 2
LAST = NH - 1
LATE = HALF - 2
ROWS = BLK + 2 * BLK // NCOL


def place(z, y):
    return (z % NZ) * NY + y % NY


def col_distance(a, b):
    ax, al, ak = a // (NL * NK), a // NK % NL, a % NK
    bx, bl, bk = b // (NL * NK), b // NK % NL, b % NK
    dx = abs(ax - bx)
    return min(dx, NX - dx) * 4 + abs(al - bl) * 4 + abs(ak - bk)


def plan():
    chosen = {}
    for t in range(NH):
        for s in range(t):
            dz, dy = (HELD[t][0] - HELD[s][0]) % NZ, (HELD[t][1] - HELD[s][1]) % NY
            if (dz, dy) not in chosen and (-dz % NZ, -dy % NY) not in chosen:
                chosen[(dz, dy)] = (s, t)
    left = np.zeros((NR, NCOL), np.int32)
    right = np.zeros((NR, NCOL), np.int32)
    sends = ([], [])
    seen = set()
    for z in range(NZ):
        for y in range(NY):
            g = place(z, y)
            early, late, either = [], [], []
            for (dz, dy), (s, t) in chosen.items():
                if (dz, dy) == (4, 0) and z >= 4 or (dz, dy) == (4, 2) and z < 4 or (dz, dy) == (0, 2) and y >= 2:
                    continue
                a = place(z + HELD[s][0], y + HELD[s][1])
                b = place(z + HELD[t][0], y + HELD[t][1])
                pair = (a, b, s, t) if a > b else (b, a, t, s)
                (either if (dz, dy) == (0, 2) else early if t < EARLY else late).append(pair)
            for pair in either:
                (early if len(early) < HALF else late).append(pair)
            late.sort(key=lambda pair: LAST in pair[2:])
            assert len(early) <= HALF and len(late) <= HALF and len(late) >= HALF - 1
            for base, todo in ((0, early), (1, late)):
                fixed = LATE if base else len(todo)
                cand = sorted(
                    (col_distance(2 * i + base, blk[0] // 2), n, i)
                    for n, blk in enumerate(todo[:fixed])
                    for i in range(LATE if base else HALF)
                )
                slot, used = {n: n for n in range(fixed, len(todo))}, set()
                for _, n, i in cand:
                    if n not in slot and i not in used:
                        slot[n] = i
                        used.add(i)
                for n, (p, q, l, r) in enumerate(todo):
                    left[g, base * HALF + slot[n]], right[g, base * HALF + slot[n]] = l, r
                    sends[p % 2].append((g * NCOL + 2 * slot[n] + base, q * NCOL + p // 2))
                    assert (p, q) not in seen
                    seen.add((p, q))
    assert len(seen) == NR * (NR - 1) // 2
    swap = np.asarray(SWAP, np.int32)
    return np.stack([left, swap[left]], 1), np.stack([right, swap[right]], 1), sends


def product(m, s):
    return lax.dot_general(m, s, (((1,), (1,)), ((), ())), preferred_element_type=jnp.float32)


def scale(m, d):
    return (m.astype(jnp.float32) * d).astype(jnp.bfloat16)


def early_kernel(left, right, d_ref, *refs):
    rows, (out, masked, scaled) = refs[:EARLY], refs[EARLY:]
    d = d_ref[...]
    for i in range(EARLY):
        m = rows[i][:BLK]
        masked[i] = m
        scaled[i] = scale(m, d)
    for c in range(HALF):
        out[c] = product(masked[left[c]], scaled[right[c]])


def late_kernel(left, right, d_ref, masked_in, scaled_in, early, riders, *refs):
    rows, (out, masked, scaled) = refs[: LAST - EARLY], refs[LAST - EARLY :]
    d = d_ref[...]
    for i in range(EARLY):
        masked[i] = masked_in[i]
        scaled[i] = scaled_in[i]
    for i in range(EARLY, LAST):
        m = rows[i - EARLY][...]
        masked[i] = m
        scaled[i] = scale(m, d)
    for c in range(HALF):
        out[2 * c, :BLK] = early[c]
    for c in range(LATE):
        out[2 * c + 1, :BLK] = product(masked[left[HALF + c]], scaled[right[HALF + c]])
    for c in range(NCOL):
        out[c, BLK:] = riders[...]


def last_kernel(left, right, d_ref, masked, scaled, row, unused, out, scaled_row):
    scaled_row[...] = scale(row[:BLK], d_ref[...])
    for c in range(LATE, HALF):
        l, r = left[HALF + c], right[HALF + c]

        @pl.when(l == LAST)
        def _():
            out[2 * c + 1, :BLK] = product(row[:BLK], scaled[r])

        @pl.when(r == LAST)
        def _():
            out[2 * c + 1, :BLK] = product(masked[l], scaled_row[...])

        @pl.when((l != LAST) & (r != LAST))
        def _():
            out[2 * c + 1, :BLK] = product(masked[l], scaled[r])


def diag_kernel(ids, period, damping, d_ref, m_ref, out):
    m = m_ref[...]
    damp = jnp.where(ids[1] == 0, damping[period[0]], 0.0)
    i = lax.broadcasted_iota(jnp.int32, (BLK, BLK), 0)
    j = lax.broadcasted_iota(jnp.int32, (BLK, BLK), 1)
    out[...] = product(m, scale(m, d_ref[...])) + jnp.where(i == j, damp, 0.0)


def final_kernel(ids, even, odd, diag, out):
    row, col = ids[0], ids[1]
    own = row // 2 == col
    out[0:BLK] = jnp.where(own & (row % 2 == 0), diag[...], even[...])
    out[BLK : 2 * BLK] = jnp.where(own & (row % 2 == 1), diag[...], odd[...])


def body(constraint, pattern, scaling, period, column_period, damping):
    left, right, sends = plan()
    row, col = lax.axis_index(ROW), lax.axis_index(COL)
    vmem = pl.BlockSpec(memory_space=pltpu.VMEM)
    smem = pl.BlockSpec(memory_space=pltpu.SMEM)

    same = column_period[None, :] == period[:, None]
    before = column_period[None, :] == period[:, None] - 1
    present = jnp.where(same | before | (pattern > 0), 1, 0).astype(constraint.dtype)
    masked = constraint * jnp.repeat(present, BLK, axis=1)

    def move(x, dz, dy):
        pairs = [
            (place(z + dz, y + (1 - 2 * k) * dy) * 2 + k, place(z, y) * 2 + k)
            for z in range(NZ)
            for y in range(NY)
            for k in range(2)
        ]
        return lax.ppermute(x, ROW + ("core",), pairs)

    longer = jnp.pad(masked, ((0, 8), (0, 0)))
    held = [masked] + [move(longer if at == HELD[1] else masked, *at) for at in HELD[1:EARLY]]
    held += [move(held[2], 1, 0), move(held[3], 0, 1), move(held[1], -1, 0)]

    small = pltpu.CompilerParams(vmem_limit_bytes=4 * 2**20)
    d = scaling.reshape(1, KC)
    ids = jnp.stack([row, col])
    diag = pl.pallas_call(
        diag_kernel,
        out_shape=jax.ShapeDtypeStruct((BLK, BLK), jnp.float32),
        in_specs=[smem] * 3 + [vmem] * 2,
        out_specs=vmem,
        compiler_params=small,
        name="diag",
    )(ids, period, damping, d, masked)
    strips = lax.all_to_all(diag, COL, 0, 0, tiled=True).reshape(NCOL, BLK // NCOL, BLK)
    strip = jnp.sum(strips, axis=0)
    high = lax.reduce_precision(strip, 5, 10)
    riders = jnp.concatenate([high, strip - high], axis=0)

    lt = lax.dynamic_slice(jnp.asarray(left), (row, lax.axis_index("core"), 0), (1, 1, NCOL)).reshape(NCOL)
    rt = lax.dynamic_slice(jnp.asarray(right), (row, lax.axis_index("core"), 0), (1, 1, NCOL)).reshape(NCOL)
    stack = jax.ShapeDtypeStruct((EARLY, BLK, KC), jnp.bfloat16)
    sums = jax.ShapeDtypeStruct((HALF, BLK, BLK), jnp.float32)
    params = pltpu.CompilerParams(vmem_limit_bytes=20 * 2**20)
    early, masked_rows, scaled_rows = pl.pallas_call(
        early_kernel,
        out_shape=(sums, stack, stack),
        in_specs=[smem] * 2 + [vmem] * (1 + EARLY),
        out_specs=(vmem,) * 3,
        compiler_params=params,
        name="early",
    )(lt, rt, d, *held[:EARLY])
    known = jax.ShapeDtypeStruct((LAST, BLK, KC), jnp.bfloat16)
    parts, masked_rows, scaled_rows = pl.pallas_call(
        late_kernel,
        out_shape=(jax.ShapeDtypeStruct((NCOL, ROWS, BLK), jnp.float32), known, known),
        in_specs=[smem] * 2 + [vmem] * (5 + LAST - EARLY),
        out_specs=(vmem,) * 3,
        compiler_params=params,
        name="late",
    )(lt, rt, d, masked_rows, scaled_rows, early, riders, *held[EARLY:LAST])
    parts = pl.pallas_call(
        last_kernel,
        out_shape=jax.ShapeDtypeStruct((NCOL, ROWS, BLK), jnp.float32),
        in_specs=[smem] * 2 + [vmem] * 5,
        out_specs=vmem,
        scratch_shapes=[pltpu.VMEM((BLK, KC), jnp.bfloat16)],
        input_output_aliases={6: 0},
        compiler_params=params,
        name="last",
    )(lt, rt, d, masked_rows, scaled_rows, held[LAST], parts)
    parts = parts.astype(jnp.float16)
    parts = lax.all_to_all(parts, COL, 0, 0, tiled=True).astype(jnp.float32)
    mine = jnp.sum(parts[:, :BLK], axis=0)
    step = BLK // NCOL
    diag = (parts[:, BLK : BLK + step] + parts[:, BLK + step :]).reshape(BLK, BLK)
    even = lax.ppermute(mine, ROW + COL, sends[0])
    odd = lax.ppermute(mine, ROW + COL, sends[1])
    return pl.pallas_call(
        final_kernel,
        out_shape=jax.ShapeDtypeStruct((2 * BLK, BLK), jnp.float32),
        in_specs=[smem] + [vmem] * 3,
        out_specs=vmem,
        compiler_params=small,
        name="final",
    )(ids, even, odd, diag)


def solution(mesh):
    split = Mesh(mesh.devices.reshape(NZ, NY, NX, NL, NK), ROW + COL)
    return jax.shard_map(
        body,
        mesh=split,
        in_specs=(P(ROW, COL), P(ROW, COL), P(COL), P(ROW), P(COL), P()),
        out_specs=P(COL, ROW),
        check_vma=False,
    )
```

```python
import jax
import jax.numpy as jnp
import numpy as np
from jax import lax
from jax.experimental import pallas as pl
from jax.experimental.pallas import tpu as pltpu
from jax.sharding import Mesh, PartitionSpec as P

ROW = ("z", "yh")
COL = ("x", "yl", "core")
NZ, NY, NX, NL, NK = 8, 4, 4, 2, 2
NR, NCOL = NZ * NY, NX * NL * NK
BLK = 128
KC = 1536

HELD = ((0, 0), (5, 0), (1, 0), (0, 1), (0, 3), (2, 0), (0, 2), (4, 0))
NH = len(HELD)
SWAP = (0, 1, 2, 4, 3, 5, 6, 7)
EARLY = 5
HALF = NCOL // 2
LAST = NH - 1
LATE = HALF - 2
ROWS = BLK + 2 * BLK // NCOL


def place(z, y):
    return (z % NZ) * NY + y % NY


def col_distance(a, b):
    ax, al, ak = a // (NL * NK), a // NK % NL, a % NK
    bx, bl, bk = b // (NL * NK), b // NK % NL, b % NK
    dx = abs(ax - bx)
    return min(dx, NX - dx) * 4 + abs(al - bl) * 4 + abs(ak - bk)


def plan():
    chosen = {}
    for t in range(NH):
        for s in range(t):
            dz, dy = (HELD[t][0] - HELD[s][0]) % NZ, (HELD[t][1] - HELD[s][1]) % NY
            if (dz, dy) not in chosen and (-dz % NZ, -dy % NY) not in chosen:
                chosen[(dz, dy)] = (s, t)
    left = np.zeros((NR, NCOL), np.int32)
    right = np.zeros((NR, NCOL), np.int32)
    sends = ([], [])
    seen = set()
    for z in range(NZ):
        for y in range(NY):
            g = place(z, y)
            early, late, either = [], [], []
            for (dz, dy), (s, t) in chosen.items():
                if (dz, dy) == (4, 0) and z >= 4 or (dz, dy) == (4, 2) and z < 4 or (dz, dy) == (0, 2) and y >= 2:
                    continue
                a = place(z + HELD[s][0], y + HELD[s][1])
                b = place(z + HELD[t][0], y + HELD[t][1])
                pair = (a, b, s, t) if a > b else (b, a, t, s)
                (either if (dz, dy) == (0, 2) else early if t < EARLY else late).append(pair)
            for pair in either:
                (early if len(early) < HALF else late).append(pair)
            late.sort(key=lambda pair: LAST in pair[2:])
            assert len(early) <= HALF and len(late) <= HALF and len(late) >= HALF - 1
            for base, todo in ((0, early), (1, late)):
                fixed = LATE if base else len(todo)
                cand = sorted(
                    (col_distance(2 * i + base, blk[0] // 2), n, i)
                    for n, blk in enumerate(todo[:fixed])
                    for i in range(LATE if base else HALF)
                )
                slot, used = {n: n for n in range(fixed, len(todo))}, set()
                for _, n, i in cand:
                    if n not in slot and i not in used:
                        slot[n] = i
                        used.add(i)
                for n, (p, q, l, r) in enumerate(todo):
                    left[g, base * HALF + slot[n]], right[g, base * HALF + slot[n]] = l, r
                    sends[p % 2].append((g * NCOL + 2 * slot[n] + base, q * NCOL + p // 2))
                    assert (p, q) not in seen
                    seen.add((p, q))
    assert len(seen) == NR * (NR - 1) // 2
    swap = np.asarray(SWAP, np.int32)
    return np.stack([left, swap[left]], 1), np.stack([right, swap[right]], 1), sends


def product(m, s):
    return lax.dot_general(m, s, (((1,), (1,)), ((), ())), preferred_element_type=jnp.float32)


def scale(m, d):
    return (m.astype(jnp.float32) * d).astype(jnp.bfloat16)


def early_kernel(left, right, d_ref, *refs):
    rows, (out, masked, scaled) = refs[:EARLY], refs[EARLY:]
    d = d_ref[...]
    for i in range(EARLY):
        m = rows[i][:BLK]
        masked[i] = m
        scaled[i] = scale(m, d)
    for c in range(HALF):
        out[c] = product(masked[left[c]], scaled[right[c]])


def late_kernel(left, right, d_ref, masked_in, scaled_in, early, riders, *refs):
    rows, (out, masked, scaled) = refs[: LAST - EARLY], refs[LAST - EARLY :]
    d = d_ref[...]
    for i in range(EARLY):
        masked[i] = masked_in[i]
        scaled[i] = scaled_in[i]
    for i in range(EARLY, LAST):
        m = rows[i - EARLY][...]
        masked[i] = m
        scaled[i] = scale(m, d)
    for c in range(HALF):
        out[2 * c, :BLK] = early[c]
    for c in range(LATE):
        out[2 * c + 1, :BLK] = product(masked[left[HALF + c]], scaled[right[HALF + c]])
    for c in range(NCOL):
        out[c, BLK:] = riders[...]


def last_kernel(left, right, d_ref, masked, scaled, row, unused, out, scaled_row):
    scaled_row[...] = scale(row[:BLK], d_ref[...])
    for c in range(LATE, HALF):
        l, r = left[HALF + c], right[HALF + c]

        @pl.when(l == LAST)
        def _():
            out[2 * c + 1, :BLK] = product(row[:BLK], scaled[r])

        @pl.when(r == LAST)
        def _():
            out[2 * c + 1, :BLK] = product(masked[l], scaled_row[...])

        @pl.when((l != LAST) & (r != LAST))
        def _():
            out[2 * c + 1, :BLK] = product(masked[l], scaled[r])


def diag_kernel(ids, period, damping, d_ref, m_ref, out):
    m = m_ref[...]
    damp = jnp.where(ids[1] == 0, damping[period[0]], 0.0)
    i = lax.broadcasted_iota(jnp.int32, (BLK, BLK), 0)
    j = lax.broadcasted_iota(jnp.int32, (BLK, BLK), 1)
    out[...] = product(m, scale(m, d_ref[...])) + jnp.where(i == j, damp, 0.0)


def body(constraint, pattern, scaling, period, column_period, damping):
    left, right, sends = plan()
    row, col = lax.axis_index(ROW), lax.axis_index(COL)
    vmem = pl.BlockSpec(memory_space=pltpu.VMEM)
    smem = pl.BlockSpec(memory_space=pltpu.SMEM)

    same = column_period[None, :] == period[:, None]
    before = column_period[None, :] == period[:, None] - 1
    present = jnp.where(same | before | (pattern > 0), 1, 0).astype(constraint.dtype)
    masked = constraint * jnp.repeat(present, BLK, axis=1)

    def move(x, dz, dy):
        pairs = [
            (place(z + dz, y + (1 - 2 * k) * dy) * 2 + k, place(z, y) * 2 + k)
            for z in range(NZ)
            for y in range(NY)
            for k in range(2)
        ]
        return lax.ppermute(x, ROW + ("core",), pairs)

    longer = jnp.pad(masked, ((0, 8), (0, 0)))
    held = [masked] + [move(longer if at == HELD[1] else masked, *at) for at in HELD[1:EARLY]]
    held += [move(held[2], 1, 0), move(held[3], 0, 1), move(held[1], -1, 0)]

    small = pltpu.CompilerParams(vmem_limit_bytes=4 * 2**20)
    d = scaling.reshape(1, KC)
    ids = jnp.stack([row, col])
    diag = pl.pallas_call(
        diag_kernel,
        out_shape=jax.ShapeDtypeStruct((BLK, BLK), jnp.float32),
        in_specs=[smem] * 3 + [vmem] * 2,
        out_specs=vmem,
        compiler_params=small,
        name="diag",
    )(ids, period, damping, d, masked)
    strips = lax.all_to_all(diag, COL, 0, 0, tiled=True).reshape(NCOL, BLK // NCOL, BLK)
    strip = jnp.sum(strips, axis=0)
    high = lax.reduce_precision(strip, 5, 10)
    riders = jnp.concatenate([high, strip - high], axis=0)

    lt = lax.dynamic_slice(jnp.asarray(left), (row, lax.axis_index("core"), 0), (1, 1, NCOL)).reshape(NCOL)
    rt = lax.dynamic_slice(jnp.asarray(right), (row, lax.axis_index("core"), 0), (1, 1, NCOL)).reshape(NCOL)
    stack = jax.ShapeDtypeStruct((EARLY, BLK, KC), jnp.bfloat16)
    sums = jax.ShapeDtypeStruct((HALF, BLK, BLK), jnp.float32)
    params = pltpu.CompilerParams(vmem_limit_bytes=20 * 2**20)
    early, masked_rows, scaled_rows = pl.pallas_call(
        early_kernel,
        out_shape=(sums, stack, stack),
        in_specs=[smem] * 2 + [vmem] * (1 + EARLY),
        out_specs=(vmem,) * 3,
        compiler_params=params,
        name="early",
    )(lt, rt, d, *held[:EARLY])
    known = jax.ShapeDtypeStruct((LAST, BLK, KC), jnp.bfloat16)
    parts, masked_rows, scaled_rows = pl.pallas_call(
        late_kernel,
        out_shape=(jax.ShapeDtypeStruct((NCOL, ROWS, BLK), jnp.float32), known, known),
        in_specs=[smem] * 2 + [vmem] * (5 + LAST - EARLY),
        out_specs=(vmem,) * 3,
        compiler_params=params,
        name="late",
    )(lt, rt, d, masked_rows, scaled_rows, early, riders, *held[EARLY:LAST])
    parts = pl.pallas_call(
        last_kernel,
        out_shape=jax.ShapeDtypeStruct((NCOL, ROWS, BLK), jnp.float32),
        in_specs=[smem] * 2 + [vmem] * 5,
        out_specs=vmem,
        scratch_shapes=[pltpu.VMEM((BLK, KC), jnp.bfloat16)],
        input_output_aliases={6: 0},
        compiler_params=params,
        name="last",
    )(lt, rt, d, masked_rows, scaled_rows, held[LAST], parts)
    parts = parts.astype(jnp.float16)
    parts = lax.all_to_all(parts, COL, 0, 0, tiled=True).astype(jnp.float32)
    mine = jnp.sum(parts[:, :BLK], axis=0)
    step = BLK // NCOL
    diag = (parts[:, BLK : BLK + step] + parts[:, BLK + step :]).reshape(BLK, BLK)
    even = lax.ppermute(mine, ROW + COL, sends[0])
    odd = lax.ppermute(mine, ROW + COL, sends[1])
    own = row // 2 == col
    halves = [jnp.where(own & (row % 2 == h), diag, block) for h, block in enumerate((even, odd))]
    return jnp.concatenate(halves, axis=0)


def solution(mesh):
    split = Mesh(mesh.devices.reshape(NZ, NY, NX, NL, NK), ROW + COL)
    return jax.shard_map(
        body,
        mesh=split,
        in_specs=(P(ROW, COL), P(ROW, COL), P(COL), P(ROW), P(COL), P()),
        out_specs=P(COL, ROW),
        check_vma=False,
    )
```

```python
import jax
import jax.numpy as jnp
import numpy as np
from jax import lax
from jax.experimental import pallas as pl
from jax.experimental.pallas import tpu as pltpu
from jax.sharding import Mesh, PartitionSpec as P

ROW = ("z", "yh")
COL = ("x", "yl", "core")
NZ, NY, NX, NL, NK = 8, 4, 4, 2, 2
NR, NCOL = NZ * NY, NX * NL * NK
BLK = 128
KC = 1536

HELD = ((0, 0), (5, 0), (1, 0), (0, 1), (0, 3), (2, 0), (0, 2), (4, 0))
NH = len(HELD)
SWAP = (0, 1, 2, 4, 3, 5, 6, 7)
EARLY = 5
HALF = NCOL // 2
LAST = NH - 1
LATE = HALF - 2
ROWS = BLK + BLK // NCOL


def place(z, y):
    return (z % NZ) * NY + y % NY


def col_distance(a, b):
    ax, al, ak = a // (NL * NK), a // NK % NL, a % NK
    bx, bl, bk = b // (NL * NK), b // NK % NL, b % NK
    dx = abs(ax - bx)
    return min(dx, NX - dx) * 4 + abs(al - bl) * 4 + abs(ak - bk)


def plan():
    chosen = {}
    for t in range(NH):
        for s in range(t):
            dz, dy = (HELD[t][0] - HELD[s][0]) % NZ, (HELD[t][1] - HELD[s][1]) % NY
            if (dz, dy) not in chosen and (-dz % NZ, -dy % NY) not in chosen:
                chosen[(dz, dy)] = (s, t)
    left = np.zeros((NR, NCOL), np.int32)
    right = np.zeros((NR, NCOL), np.int32)
    sends = ([], [])
    seen = set()
    for z in range(NZ):
        for y in range(NY):
            g = place(z, y)
            early, late, either = [], [], []
            for (dz, dy), (s, t) in chosen.items():
                if (dz, dy) == (4, 0) and z >= 4 or (dz, dy) == (4, 2) and z < 4 or (dz, dy) == (0, 2) and y >= 2:
                    continue
                a = place(z + HELD[s][0], y + HELD[s][1])
                b = place(z + HELD[t][0], y + HELD[t][1])
                pair = (a, b, s, t) if a > b else (b, a, t, s)
                (either if (dz, dy) == (0, 2) else early if t < EARLY else late).append(pair)
            for pair in either:
                (early if len(early) < HALF else late).append(pair)
            late.sort(key=lambda pair: LAST in pair[2:])
            assert len(early) <= HALF and len(late) <= HALF and len(late) >= HALF - 1
            for base, todo in ((0, early), (1, late)):
                fixed = LATE if base else len(todo)
                cand = sorted(
                    (col_distance(2 * i + base, blk[0] // 2), n, i)
                    for n, blk in enumerate(todo[:fixed])
                    for i in range(LATE if base else HALF)
                )
                slot, used = {n: n for n in range(fixed, len(todo))}, set()
                for _, n, i in cand:
                    if n not in slot and i not in used:
                        slot[n] = i
                        used.add(i)
                for n, (p, q, l, r) in enumerate(todo):
                    left[g, base * HALF + slot[n]], right[g, base * HALF + slot[n]] = l, r
                    sends[p % 2].append((g * NCOL + 2 * slot[n] + base, q * NCOL + p // 2))
                    assert (p, q) not in seen
                    seen.add((p, q))
    assert len(seen) == NR * (NR - 1) // 2
    swap = np.asarray(SWAP, np.int32)
    return np.stack([left, swap[left]], 1), np.stack([right, swap[right]], 1), sends


def product(m, s):
    return lax.dot_general(m, s, (((1,), (1,)), ((), ())), preferred_element_type=jnp.float32)


def scale(m, d):
    return (m.astype(jnp.float32) * d).astype(jnp.bfloat16)


def early_kernel(left, right, d_ref, *refs):
    rows, (out, masked, scaled) = refs[:EARLY], refs[EARLY:]
    d = d_ref[...]
    for i in range(EARLY):
        m = rows[i][:BLK]
        masked[i] = m
        scaled[i] = scale(m, d)
    for c in range(HALF):
        out[c] = product(masked[left[c]], scaled[right[c]])


def late_kernel(left, right, d_ref, masked_in, scaled_in, early, riders, *refs):
    rows, (out, masked, scaled) = refs[: LAST - EARLY], refs[LAST - EARLY :]
    d = d_ref[...]
    for i in range(EARLY):
        masked[i] = masked_in[i]
        scaled[i] = scaled_in[i]
    for i in range(EARLY, LAST):
        m = rows[i - EARLY][...]
        masked[i] = m
        scaled[i] = scale(m, d)
    for c in range(HALF):
        out[2 * c, :BLK] = early[c]
    for c in range(LATE):
        out[2 * c + 1, :BLK] = product(masked[left[HALF + c]], scaled[right[HALF + c]])
    for c in range(NCOL):
        out[c, BLK:] = riders[: BLK // NCOL]


def last_kernel(left, right, d_ref, masked, scaled, row, unused, out, scaled_row):
    scaled_row[...] = scale(row[:BLK], d_ref[...])
    for c in range(LATE, HALF):
        l, r = left[HALF + c], right[HALF + c]

        @pl.when(l == LAST)
        def _():
            out[2 * c + 1, :BLK] = product(row[:BLK], scaled[r])

        @pl.when(r == LAST)
        def _():
            out[2 * c + 1, :BLK] = product(masked[l], scaled_row[...])

        @pl.when((l != LAST) & (r != LAST))
        def _():
            out[2 * c + 1, :BLK] = product(masked[l], scaled[r])


def diag_kernel(ids, period, damping, d_ref, m_ref, out):
    m = m_ref[...]
    damp = jnp.where(ids[1] == 0, damping[period[0]], 0.0)
    i = lax.broadcasted_iota(jnp.int32, (BLK, BLK), 0)
    j = lax.broadcasted_iota(jnp.int32, (BLK, BLK), 1)
    out[...] = product(m, scale(m, d_ref[...])) + jnp.where(i == j, damp, 0.0)


def body(constraint, pattern, scaling, period, column_period, damping):
    left, right, sends = plan()
    row, col = lax.axis_index(ROW), lax.axis_index(COL)
    vmem = pl.BlockSpec(memory_space=pltpu.VMEM)
    smem = pl.BlockSpec(memory_space=pltpu.SMEM)

    same = column_period[None, :] == period[:, None]
    before = column_period[None, :] == period[:, None] - 1
    present = jnp.where(same | before | (pattern > 0), 1, 0).astype(constraint.dtype)
    masked = constraint * jnp.repeat(present, BLK, axis=1)

    def move(x, dz, dy):
        pairs = [
            (place(z + dz, y + (1 - 2 * k) * dy) * 2 + k, place(z, y) * 2 + k)
            for z in range(NZ)
            for y in range(NY)
            for k in range(2)
        ]
        return lax.ppermute(x, ROW + ("core",), pairs)

    longer = jnp.pad(masked, ((0, 8), (0, 0)))
    held = [masked] + [move(longer if at == HELD[1] else masked, *at) for at in HELD[1:EARLY]]
    held += [move(held[2], 1, 0), move(held[3], 0, 1), move(held[1], -1, 0)]

    small = pltpu.CompilerParams(vmem_limit_bytes=4 * 2**20)
    d = scaling.reshape(1, KC)
    ids = jnp.stack([row, col])
    diag = pl.pallas_call(
        diag_kernel,
        out_shape=jax.ShapeDtypeStruct((BLK, BLK), jnp.float32),
        in_specs=[smem] * 3 + [vmem] * 2,
        out_specs=vmem,
        compiler_params=small,
        name="diag",
    )(ids, period, damping, d, masked)
    strips = lax.all_to_all(diag, COL, 0, 0, tiled=True).reshape(NCOL, BLK // NCOL, BLK)
    strip = jnp.sum(strips, axis=0)
    high = lax.reduce_precision(strip, 5, 10)
    riders = jnp.concatenate([high, strip - high], axis=0)

    lt = lax.dynamic_slice(jnp.asarray(left), (row, lax.axis_index("core"), 0), (1, 1, NCOL)).reshape(NCOL)
    rt = lax.dynamic_slice(jnp.asarray(right), (row, lax.axis_index("core"), 0), (1, 1, NCOL)).reshape(NCOL)
    stack = jax.ShapeDtypeStruct((EARLY, BLK, KC), jnp.bfloat16)
    sums = jax.ShapeDtypeStruct((HALF, BLK, BLK), jnp.float32)
    params = pltpu.CompilerParams(vmem_limit_bytes=20 * 2**20)
    early, masked_rows, scaled_rows = pl.pallas_call(
        early_kernel,
        out_shape=(sums, stack, stack),
        in_specs=[smem] * 2 + [vmem] * (1 + EARLY),
        out_specs=(vmem,) * 3,
        compiler_params=params,
        name="early",
    )(lt, rt, d, *held[:EARLY])
    known = jax.ShapeDtypeStruct((LAST, BLK, KC), jnp.bfloat16)
    parts, masked_rows, scaled_rows = pl.pallas_call(
        late_kernel,
        out_shape=(jax.ShapeDtypeStruct((NCOL, ROWS, BLK), jnp.float32), known, known),
        in_specs=[smem] * 2 + [vmem] * (5 + LAST - EARLY),
        out_specs=(vmem,) * 3,
        compiler_params=params,
        name="late",
    )(lt, rt, d, masked_rows, scaled_rows, early, riders, *held[EARLY:LAST])
    parts = pl.pallas_call(
        last_kernel,
        out_shape=jax.ShapeDtypeStruct((NCOL, ROWS, BLK), jnp.float32),
        in_specs=[smem] * 2 + [vmem] * 5,
        out_specs=vmem,
        scratch_shapes=[pltpu.VMEM((BLK, KC), jnp.bfloat16)],
        input_output_aliases={6: 0},
        compiler_params=params,
        name="last",
    )(lt, rt, d, masked_rows, scaled_rows, held[LAST], parts)
    parts = parts.astype(jnp.float16)
    parts = lax.all_to_all(parts, COL, 0, 0, tiled=True).astype(jnp.float32)
    mine = jnp.sum(parts[:, :BLK], axis=0)
    diag = parts[:, BLK:].reshape(BLK, BLK)
    even = lax.ppermute(mine, ROW + COL, sends[0])
    odd = lax.ppermute(mine, ROW + COL, sends[1])
    own = row // 2 == col
    halves = [jnp.where(own & (row % 2 == h), diag, block) for h, block in enumerate((even, odd))]
    return jnp.concatenate(halves, axis=0)


def solution(mesh):
    split = Mesh(mesh.devices.reshape(NZ, NY, NX, NL, NK), ROW + COL)
    return jax.shard_map(
        body,
        mesh=split,
        in_specs=(P(ROW, COL), P(ROW, COL), P(COL), P(ROW), P(COL), P()),
        out_specs=P(COL, ROW),
        check_vma=False,
    )
```
